32 devices in a mesh: blk: 16 (over z, x, core), uly: 2 (over y).
Axes of the slice: x: 2, y: 2, z: 4, core: 2. Of those that a mesh axis runs over, the one named last changes fastest.
Arguments:
- queries: bfloat16 [16384, 1024], P(('blk', 'uly')), may hold values from -6 to 6
- key_states: bfloat16 [16384, 128], P(('blk', 'uly')), may hold values from -6 to 6
- value_states: bfloat16 [16384, 128], P(('blk', 'uly')), may hold values from -6 to 6
- attn_output: bfloat16 [16384, 1024], P(('blk', 'uly')), may hold values from -6 to 6
- grad_output: bfloat16 [16384, 1024], P(('blk', 'uly')), may hold values from -6 to 6
- log_normalizer: float32 [8, 16384], P(None, ('blk', 'uly')), may hold values from 0 to 12
- span_order: int32 [32], replicated, may hold values from 0 to 31, as said below
Outputs:
- grad_queries: bfloat16 [16384, 1024], P(('blk', 'uly'))
- grad_keys: bfloat16 [16384, 128], P(('blk', 'uly'))
- grad_values: bfloat16 [16384, 128], P(('blk', 'uly'))
The draws below stay inside these ranges and needn't reach their ends.
Inputs may be any that keep to these rules, and one draw needn't show every extreme that they name: `span_order`: every value appears once; for every b, entries 2b and 2b+1 lie in sequence b mod 1 (value // 32) and sum to (2 * (b mod 1) + 1) * 2 * 16 - 1.
All inputs are finite; a program needn't handle non-finite values.
Results may differ from the reference program's by a relative error of at most 0.0051.
Values may be sent and summed in bfloat16 or wider, within the bound.
A program may use at most 64 MiB of HBM per device.

```python
import math
import jax
import jax.numpy as jnp
from jax import lax

HQ = 8
DH = 128
CYCLE = 16
SPAN = 512
SEQS = 1
SEQ = 16384
TOTAL = 16384
NCHUNK = 32
N_BLK = 16


def paired_order(key):
    groups = jnp.arange(N_BLK, dtype=jnp.int32)
    sequence = groups % SEQS
    slot = groups // SEQS
    seq_keys = jax.random.split(jax.random.fold_in(key, 11), SEQS)
    perms = jax.vmap(lambda one_key: jax.random.permutation(one_key, CYCLE))(seq_keys).astype(jnp.int32)
    permuted = perms[sequence, slot].astype(jnp.int32)
    flipped = jax.random.randint(jax.random.fold_in(key, 12), (N_BLK,), 0, 2).astype(jnp.int32)
    mirrored = 2 * CYCLE - 1 - permuted
    offset = sequence * 2 * CYCLE
    first_part = flipped * permuted + (1 - flipped) * mirrored + offset
    second_part = flipped * mirrored + (1 - flipped) * permuted + offset
    return jnp.stack([first_part, second_part], axis=1).reshape(NCHUNK).astype(jnp.int32)


def draw_span_order(key, part):
    return paired_order(key)


def draw_log_normalizer(key, part):
    ordering = paired_order(key)
    storage = jnp.arange(TOTAL, dtype=jnp.int32)
    position = (ordering[storage // SPAN] * SPAN + storage % SPAN) % SEQ
    base_value = jnp.log(position.astype(jnp.float32) + 1.0)
    offsets = jax.random.uniform(jax.random.fold_in(key, 21), (HQ, TOTAL), jnp.float32, 0.0, 1.0)
    return (base_value[None, :] + offsets).astype(jnp.float32)


def block_scale(own_key, extent, cuts, low, high):
    def one(axis_at, shards_of):
        heights = jax.random.uniform(jax.random.fold_in(jax.random.fold_in(own_key, 6), axis_at), (shards_of,), jnp.float32, low / len(cuts), high / len(cuts))
        return jnp.repeat(jnp.exp(heights), extent[axis_at] // shards_of).reshape((-1,) + (1,) * (len(extent) - axis_at - 1))

    gain = one(*cuts[0])
    for cut in cuts[1:]:
        gain = gain * one(*cut)
    return gain


def scatter_about(key, extent, spread, limit, cuts=(), kind=jnp.bfloat16):
    result = spread * jax.random.normal(key, extent, jnp.float32)
    if cuts:
        result = result * block_scale(key, extent, cuts, -0.22, 0.18)
    return jnp.clip(result, -limit, limit).astype(kind)


def setup_inputs(seed: int = 0) -> dict:
    seeds = jax.random.split(jax.random.key(seed), 8)
    queries = scatter_about(seeds[0], (TOTAL, HQ * DH), 1.0, 6.0, ((0, 32),))
    key_states = scatter_about(seeds[1], (TOTAL, DH), 1.0, 6.0, ((0, 32),))
    value_states = scatter_about(seeds[2], (TOTAL, DH), 1.0, 6.0, ((0, 32),))
    attn_output = scatter_about(seeds[3], (TOTAL, HQ * DH), 1.0, 6.0, ((0, 32),))
    grad_output = scatter_about(seeds[4], (TOTAL, HQ * DH), 1.0, 6.0, ((0, 32),))
    log_normalizer = draw_log_normalizer(jax.random.fold_in(seeds[7], 71), 0)
    span_order = draw_span_order(jax.random.fold_in(seeds[7], 71), 0)
    return {"queries": queries, "key_states": key_states, "value_states": value_states, "attn_output": attn_output, "grad_output": grad_output, "log_normalizer": log_normalizer, "span_order": span_order}


def positions_of(span_order):
    storage = jnp.arange(TOTAL, dtype=jnp.int32)
    table = span_order[storage // SPAN]
    return (table * SPAN + storage % SPAN).astype(jnp.int32)

def reference(queries, key_states, value_states, attn_output, grad_output, log_normalizer, span_order):
    scaling = 1.0 / math.sqrt(DH)
    position = positions_of(span_order)
    out_heads = attn_output.reshape(TOTAL, HQ, DH).astype(jnp.float32)
    grad_heads = grad_output.reshape(TOTAL, HQ, DH).astype(jnp.float32)
    delta_rows = lax.optimization_barrier(jnp.sum(out_heads * grad_heads, axis=2)).T
    block_len = 2 * SPAN
    block_count = TOTAL // block_len
    keys_split = key_states.reshape(CYCLE, SEQS, block_len, DH)
    values_split = value_states.reshape(CYCLE, SEQS, block_len, DH)
    position_split = position.reshape(CYCLE, SEQS, block_len)

    def per_head(carry, head):
        q_head = lax.dynamic_slice_in_dim(queries, head * DH, DH, 1)
        dout_head = lax.dynamic_slice_in_dim(grad_output, head * DH, DH, 1)
        lse_head = lax.dynamic_index_in_dim(log_normalizer, head, 0, keepdims=False)
        delta_head = lax.dynamic_index_in_dim(delta_rows, head, 0, keepdims=False)

        def per_block(inner, block):
            grad_keys, grad_vals = inner
            start = block * block_len
            sequence = (block % SEQS).astype(jnp.int32)
            seq_keys = lax.dynamic_index_in_dim(keys_split, sequence, 1, keepdims=False).reshape(CYCLE * block_len, DH)
            seq_values = lax.dynamic_index_in_dim(values_split, sequence, 1, keepdims=False).reshape(CYCLE * block_len, DH)
            seq_position = lax.dynamic_index_in_dim(position_split, sequence, 1, keepdims=False).reshape(CYCLE * block_len)
            q_rows = lax.dynamic_slice_in_dim(q_head, start, block_len, 0)
            d_rows = lax.dynamic_slice_in_dim(dout_head, start, block_len, 0)
            lse_rows = lax.dynamic_slice_in_dim(lse_head, start, block_len, 0)
            delta_part = lax.dynamic_slice_in_dim(delta_head, start, block_len, 0)
            q_position = lax.dynamic_slice_in_dim(position, start, block_len, 0)
            scores = jnp.dot(q_rows, seq_keys.T, preferred_element_type=jnp.float32) * scaling
            allowed = q_position[:, None] >= seq_position[None, :]
            probs = jnp.where(allowed, jnp.exp(scores - lse_rows[:, None]), 0.0)
            dprobs = jnp.dot(d_rows, seq_values.T, preferred_element_type=jnp.float32)
            dscores = (scaling * probs * (dprobs - delta_part[:, None])).astype(jnp.bfloat16)
            prob_low = probs.astype(jnp.bfloat16)
            grad_q = jnp.dot(dscores, seq_keys, preferred_element_type=jnp.float32)
            key_term = jnp.dot(dscores.T, q_rows, preferred_element_type=jnp.float32).reshape(CYCLE, block_len, DH)
            value_term = jnp.dot(prob_low.T, d_rows, preferred_element_type=jnp.float32).reshape(CYCLE, block_len, DH)
            key_now = lax.dynamic_index_in_dim(grad_keys, sequence, 1, keepdims=False) + key_term
            value_now = lax.dynamic_index_in_dim(grad_vals, sequence, 1, keepdims=False) + value_term
            grad_keys = lax.dynamic_update_index_in_dim(grad_keys, key_now, sequence, 1)
            grad_vals = lax.dynamic_update_index_in_dim(grad_vals, value_now, sequence, 1)
            return ((grad_keys, grad_vals), grad_q)
        carry, dq_blocks = lax.scan(per_block, carry, jnp.arange(block_count, dtype=jnp.int32))
        return (carry, dq_blocks.reshape(TOTAL, DH))
    zero_rows = jnp.zeros((CYCLE, SEQS, block_len, DH), jnp.float32)
    (grad_keys, grad_vals), dq_heads = lax.scan(per_head, (zero_rows, zero_rows), jnp.arange(HQ, dtype=jnp.int32))
    grad_queries = dq_heads.astype(jnp.bfloat16).transpose(1, 0, 2).reshape(TOTAL, HQ * DH)
    return (grad_queries, grad_keys.reshape(TOTAL, DH).astype(jnp.bfloat16), grad_vals.reshape(TOTAL, DH).astype(jnp.bfloat16))
```

```python
import functools
import math

import jax
import jax.numpy as jnp
from jax import lax
from jax.experimental import pallas as pl
from jax.experimental.pallas import tpu as pltpu
from jax.sharding import PartitionSpec as P

CYCLE = 16
SUB = 256
CHUNKS = 2
ORDER_A = (2, 4, 1, 8, 16)
ORDER_B = (2, 1, 8, 16, 4)
BOTH = ("blk", "uly")


def dot(a, b):
    return lax.dot_general(a, b, (((1,), (0,)), ((), ())), preferred_element_type=jnp.float32)


def tile_kernel(
    heads, span, head_dim, plan, kv_ref, qt_ref, dt_ref, q_ref, do_ref, lse_ref, delta_ref, dqi_ref, da_ref, db_ref, dq_ref
):
    step = pl.program_id(0)
    rows = kv_ref.shape[0]
    half = rows // 2
    scaling = 1.0 / math.sqrt(head_dim)
    to_log2 = math.log2(math.e) * scaling
    sub = min(SUB, span)

    @pl.when(step == 0)
    def _():
        dq_ref[...] = dqi_ref[...]

    def tile(part, diagonal):
        key = kv_ref[:, :head_dim]
        value = kv_ref[:, head_dim:]
        key_t = key.T
        dk = jnp.zeros((rows, head_dim), jnp.float32)
        dv = jnp.zeros((rows, head_dim), jnp.float32)
        for h in range(heads):
            hs = slice(h * head_dim, (h + 1) * head_dim)
            for s in range(span // sub):
                qs = slice(part * span + s * sub, part * span + (s + 1) * sub)
                scores = dot(key, qt_ref[hs, qs])
                dprobs = dot(value, dt_ref[hs, qs])
                probs = jnp.exp2(scores * to_log2 - lse_ref[h : h + 1, qs])
                if diagonal:
                    q_at = lax.broadcasted_iota(jnp.int32, (rows, sub), 1) + s * sub
                    k_at = lax.broadcasted_iota(jnp.int32, (rows, sub), 0) + plan[2, step]
                    probs = jnp.where(q_at >= k_at, probs, 0.0)
                dscores = (scaling * probs * (dprobs - delta_ref[h : h + 1, qs])).astype(jnp.bfloat16)
                dv = dv + dot(probs.astype(jnp.bfloat16), do_ref[qs, hs])
                dk = dk + dot(dscores, q_ref[qs, hs])
                dq_ref[hs, qs] += dot(key_t, dscores)
        return jnp.concatenate([dk, dv], axis=1)

    def put(total):
        da_ref[...] = total[:half].astype(da_ref.dtype)
        db_ref[...] = total[half:].astype(db_ref.dtype)

    da_ref[...] = jnp.zeros_like(da_ref)
    db_ref[...] = jnp.zeros_like(db_ref)
    for part in range(2):
        for kind in (1, 2):

            @pl.when(plan[part, step] == kind)
            def _():
                so_far = jnp.concatenate([da_ref[...], db_ref[...]], axis=0).astype(jnp.float32)
                put(so_far + tile(part, kind == 1))


def attend(plan, kv, rows, q_t, d_t, q, do, lse, delta, dq_in, span, kind):
    heads = lse.shape[0]
    head_dim = kv.shape[1] // 2
    blocks = kv.shape[0] // rows
    whole = lambda a: pl.BlockSpec(a.shape, lambda n, plan: (0, 0))
    ops = (q_t, d_t, q, do, lse, delta, dq_in)
    out = jax.ShapeDtypeStruct((kv.shape[0] // 2, 2 * head_dim), kind)
    work = 10 * 2 * span * heads * head_dim * kv.shape[0]
    return pl.pallas_call(
        functools.partial(tile_kernel, heads, span, head_dim),
        grid_spec=pltpu.PrefetchScalarGridSpec(
            num_scalar_prefetch=1,
            grid=(blocks,),
            in_specs=[pl.BlockSpec((rows, 2 * head_dim), lambda n, plan: (plan[3, n], 0))] + [whole(a) for a in ops],
            out_specs=[
                pl.BlockSpec((rows // 2, 2 * head_dim), lambda n, plan: (n, 0)),
                pl.BlockSpec((rows // 2, 2 * head_dim), lambda n, plan: (plan[4, n], 0)),
                whole(dq_in),
            ],
        ),
        out_shape=[out, out, jax.ShapeDtypeStruct(dq_in.shape, jnp.float32)],
        compiler_params=pltpu.CompilerParams(vmem_limit_bytes=48 * 2**20),
        cost_estimate=pl.CostEstimate(flops=work, bytes_accessed=4 * kv.size, transcendentals=0),
    )(plan, kv, *ops)


def swap(value, mask):
    if mask == 1:
        return lax.ppermute(value, "uly", [(0, 1), (1, 0)])
    count = lax.axis_size("blk")
    return lax.ppermute(value, "blk", [(b, b ^ (mask // 2)) for b in range(count)])


def halve(parts, order):
    keep = parts
    for mask in order:
        half = keep.shape[0] // 2
        sent = swap(keep[half:].astype(jnp.bfloat16), mask)
        keep = keep[:half].astype(jnp.float32) + sent.astype(jnp.float32)
    return keep


def spot(order, mask):
    bits = len(order)
    return sum(1 << (bits - 1 - i) for i, m in enumerate(order) if mask & m)


def body(queries, key_states, value_states, attn_output, grad_output, log_normalizer, span_order):
    local = queries.shape[0]
    heads = log_normalizer.shape[0]
    head_dim = key_states.shape[1]
    n_blk, n_uly = lax.axis_size("blk"), lax.axis_size("uly")
    count = n_blk * n_uly
    span = local * n_uly // 2
    seq_spans = span_order.shape[0] // (n_blk // CYCLE)
    folding = n_uly == 2 and n_blk == 16
    chunks = CHUNKS
    rows = local // chunks
    kv_local = jnp.concatenate([key_states, value_states], axis=1)
    kvs = [lax.all_gather(kv_local[c * rows : (c + 1) * rows], BOTH, axis=0, tiled=True) for c in range(chunks)]

    delta_local = jnp.sum(
        (attn_output.astype(jnp.float32) * grad_output.astype(jnp.float32)).reshape(local, heads, head_dim), axis=2
    ).T
    q = lax.all_to_all(queries, "uly", split_axis=1, concat_axis=0, tiled=True)
    do = lax.all_to_all(grad_output, "uly", split_axis=1, concat_axis=0, tiled=True)
    rows_in = jnp.stack([log_normalizer * math.log2(math.e), delta_local], axis=1)
    rows_group = lax.all_to_all(rows_in, "uly", split_axis=0, concat_axis=2, tiled=True)
    lse, delta = rows_group[:, 0], rows_group[:, 1]

    me = lax.axis_index("blk")
    mine = lax.dynamic_slice(span_order, (2 * me,), (2,))
    if folding:
        masks = [0] * count
        for mask in range(count):
            masks[spot(ORDER_A, mask)] = mask
        device = (me * n_uly + lax.axis_index("uly")) ^ jnp.array(masks, jnp.int32)
        second = jnp.array([spot(ORDER_B, mask) for mask in masks], jnp.int32)
    else:
        device = jnp.arange(count, dtype=jnp.int32)
        second = device
    start = (device % n_uly) * local
    block_span = span_order[2 * (device // n_uly) + start // span]
    same = (block_span // seq_spans)[None] == (mine // seq_spans)[:, None]
    order = jnp.where(mine[:, None] > block_span[None], 2, jnp.where(mine[:, None] == block_span[None], 1, 0))
    order = jnp.where(same, order, 0)

    q_t, d_t = q.T, do.T
    dq_t = jnp.zeros((q.shape[1], q.shape[0]), jnp.float32)
    totals = []
    for c in range(chunks):
        plan = jnp.concatenate([order, jnp.stack([start % span + c * rows, device, second])], axis=0).astype(jnp.int32)
        first, other, dq_t = attend(
            plan, kvs[c], rows, q_t, d_t, q, do, lse, delta, dq_t, span, jnp.bfloat16 if folding else jnp.float32
        )
        if folding:
            split = (count, rows // 2, 2 * head_dim)
            totals.append(halve(first.reshape(split), ORDER_A)[0])
            totals.append(halve(other.reshape(split), ORDER_B)[0])
        else:
            totals.append(lax.psum_scatter(first, BOTH, scatter_dimension=0, tiled=True))
            totals.append(lax.psum_scatter(other, BOTH, scatter_dimension=0, tiled=True))
    grad_queries = lax.all_to_all(dq_t.T.astype(jnp.bfloat16), "uly", split_axis=0, concat_axis=1, tiled=True)
    total = jnp.concatenate(totals, axis=0).astype(jnp.bfloat16)
    return (grad_queries, total[:, :head_dim], total[:, head_dim:])


def solution(mesh):
    return jax.shard_map(
        body,
        mesh=mesh,
        in_specs=(
            P(BOTH, None),
            P(BOTH, None),
            P(BOTH, None),
            P(BOTH, None),
            P(BOTH, None),
            P(None, BOTH),
            P(),
        ),
        out_specs=(P(BOTH, None), P(BOTH, None), P(BOTH, None)),
        check_vma=False,
    )
```

```python
import functools
import math

import jax
import jax.numpy as jnp
from jax import lax
from jax.experimental import pallas as pl
from jax.experimental.pallas import tpu as pltpu
from jax.sharding import PartitionSpec as P

CYCLE = 16
SUB = 256
ORDER = (2, 4, 1)
TURNS = (1, 2, 3, 0)
BOTH = ("blk", "uly")


def dot(a, b):
    return lax.dot_general(a, b, (((1,), (0,)), ((), ())), preferred_element_type=jnp.float32)


def tile_kernel(
    heads, span, head_dim, apart, plan, kv_ref, qt_ref, dt_ref, q_ref, do_ref, lse_ref, delta_ref, dqi_ref, *refs
):
    dq_ref, acc = refs[-2:]
    dkv_refs = refs[-2 - apart : -2]
    step = pl.program_id(0)
    rows = kv_ref.shape[0]
    scaling = 1.0 / math.sqrt(head_dim)
    to_log2 = math.log2(math.e) * scaling
    sub = min(SUB, span)

    @pl.when(step == 0)
    def _():
        dq_ref[...] = dqi_ref[...]

    def tile(part, diagonal):
        key = kv_ref[:, :head_dim]
        value = kv_ref[:, head_dim:]
        key_t = key.T
        dk = jnp.zeros((rows, head_dim), jnp.float32)
        dv = jnp.zeros((rows, head_dim), jnp.float32)
        for h in range(heads):
            hs = slice(h * head_dim, (h + 1) * head_dim)
            for s in range(span // sub):
                qs = slice(part * span + s * sub, part * span + (s + 1) * sub)
                scores = dot(key, qt_ref[hs, qs])
                dprobs = dot(value, dt_ref[hs, qs])
                probs = jnp.exp2(scores * to_log2 - lse_ref[h : h + 1, qs])
                if diagonal:
                    q_at = lax.broadcasted_iota(jnp.int32, (rows, sub), 1) + s * sub
                    k_at = lax.broadcasted_iota(jnp.int32, (rows, sub), 0) + plan[2, step]
                    probs = jnp.where(q_at >= k_at, probs, 0.0)
                dscores = (scaling * probs * (dprobs - delta_ref[h : h + 1, qs])).astype(jnp.bfloat16)
                dv = dv + dot(probs.astype(jnp.bfloat16), do_ref[qs, hs])
                dk = dk + dot(dscores, q_ref[qs, hs])
                dq_ref[hs, qs] += dot(key_t, dscores)
        acc[:, :head_dim] += dk
        acc[:, head_dim:] += dv

    acc[...] = jnp.zeros_like(acc)
    for part in range(2):
        for kind in (1, 2):

            @pl.when(plan[part, step] == kind)
            def _():
                tile(part, kind == 1)

    if apart == 1:
        dkv_refs[0][...] = acc[...].astype(dkv_refs[0].dtype)
    else:
        for n in range(apart):

            @pl.when(step == n)
            def _():
                dkv_refs[n][...] = acc[...].astype(dkv_refs[n].dtype)


def attend(plan, kv, rows, q_t, d_t, q, do, lse, delta, dq_in, span, apart, kind, after=()):
    heads = lse.shape[0]
    head_dim = kv.shape[1] // 2
    blocks = kv.shape[0] // rows
    whole = lambda a: pl.BlockSpec(a.shape, lambda n, plan: (0, 0))
    ops = (q_t, d_t, q, do, lse, delta, dq_in)
    kv_shape = (rows, 2 * head_dim)
    if apart == 1:
        kv_out = [pl.BlockSpec(kv_shape, lambda n, plan: (n, 0))]
        kv_shape = kv.shape
    else:
        kv_out = [pl.BlockSpec(kv_shape, lambda n, plan: (0, 0))] * apart
    work = 10 * 2 * span * heads * head_dim * kv.shape[0]
    return pl.pallas_call(
        functools.partial(tile_kernel, heads, span, head_dim, apart),
        grid_spec=pltpu.PrefetchScalarGridSpec(
            num_scalar_prefetch=1,
            grid=(blocks,),
            in_specs=[pl.BlockSpec((rows, 2 * head_dim), lambda n, plan: (plan[3, n], 0))]
            + [whole(a) for a in ops]
            + [pl.BlockSpec(memory_space=pl.ANY) for _ in after],
            out_specs=kv_out + [whole(dq_in)],
            scratch_shapes=[pltpu.VMEM((rows, 2 * head_dim), jnp.float32)],
        ),
        out_shape=[jax.ShapeDtypeStruct(kv_shape, kind)] * apart + [jax.ShapeDtypeStruct(dq_in.shape, jnp.float32)],
        compiler_params=pltpu.CompilerParams(vmem_limit_bytes=48 * 2**20),
        cost_estimate=pl.CostEstimate(flops=work, bytes_accessed=4 * kv.size, transcendentals=0),
    )(plan, kv, *ops, *after)


def swap(value, mask):
    count, sides = lax.axis_size("blk"), lax.axis_size("uly")
    return lax.ppermute(value, BOTH, [(d, d ^ mask) for d in range(count * sides)])


def make_plan(device, mine, span_order, local, span, spot):
    n_blk, n_uly = lax.axis_size("blk"), lax.axis_size("uly")
    seq_spans = span_order.shape[0] // (n_blk // CYCLE)
    start = (device % n_uly) * local
    block_span = span_order[2 * (device // n_uly) + start // span]
    same = (block_span // seq_spans)[None] == (mine // seq_spans)[:, None]
    order = jnp.where(mine[:, None] > block_span[None], 2, jnp.where(mine[:, None] == block_span[None], 1, 0))
    order = jnp.where(same, order, 0)
    return jnp.concatenate([order, jnp.stack([start % span, spot])], axis=0).astype(jnp.int32)


def body(queries, key_states, value_states, attn_output, grad_output, log_normalizer, span_order):
    local = queries.shape[0]
    heads = log_normalizer.shape[0]
    head_dim = key_states.shape[1]
    n_blk, n_uly = lax.axis_size("blk"), lax.axis_size("uly")
    count = n_blk * n_uly
    span = local * n_uly // 2
    plane = 2 ** len(ORDER)
    folding = n_uly == 2 and n_blk == 16
    me, side = lax.axis_index("blk"), lax.axis_index("uly")
    delta_local = jnp.sum(
        (attn_output.astype(jnp.float32) * grad_output.astype(jnp.float32)).reshape(local, heads, head_dim), axis=2
    ).T
    rows_in = jnp.stack([log_normalizer * math.log2(math.e), delta_local], axis=1)
    kv_local = jnp.concatenate([key_states, value_states], axis=1)
    pair = lax.dynamic_slice(span_order, (2 * me,), (2,))

    if folding:
        groups = [list(range(g, g + plane // 2)) for g in range(0, n_blk, plane // 2)]

        kv_pair = jnp.concatenate([kv_local, swap(kv_local, 1)], axis=0)

        def gather(k):
            block = swap(kv_pair, k * plane) if k else kv_pair
            return lax.all_gather(block, "blk", axis=0, tiled=True, axis_index_groups=groups)

        kvs = [gather(k) for k in TURNS]

        def share(value, axis):
            size = value.shape[axis] // 2
            own = lax.dynamic_slice_in_dim(value, side * size, size, axis)
            other = swap(lax.dynamic_slice_in_dim(value, (1 - side) * size, size, axis), 1)
            return own, other

        lines = jnp.concatenate(share(rows_in, 0), axis=2)
        q = jnp.concatenate(share(queries, 1), axis=0)
        do = jnp.concatenate(share(grad_output, 1), axis=0)
        mine = jnp.where(side == 0, pair, pair[::-1])
    else:
        q = lax.all_to_all(queries, "uly", split_axis=1, concat_axis=0, tiled=True)
        do = lax.all_to_all(grad_output, "uly", split_axis=1, concat_axis=0, tiled=True)
        lines = lax.all_to_all(rows_in, "uly", split_axis=0, concat_axis=2, tiled=True)
        mine = pair
    lse, delta = lines[:, 0], lines[:, 1]
    q_t, d_t = q.T, do.T
    dq_t = jnp.zeros((q.shape[1], q.shape[0]), jnp.float32)

    if folding:
        masks = [sum(m for i, m in enumerate(reversed(ORDER)) if n >> i & 1) for n in range(plane)]
        here = me * n_uly + side
        sums = []
        for turn, (k, kv) in enumerate(zip(TURNS, kvs)):
            device = here ^ (jnp.array(masks, jnp.int32) | (k * plane))
            plan = make_plan(device, mine, span_order, local, span, (device % plane) ^ side)
            after = tuple(sums[: turn - 1][-1:]) if turn > 1 else ()
            *parts, dq_t = attend(
                plan, kv, local, q_t, d_t, q, do, lse, delta, dq_t, span, plane, jnp.bfloat16, after
            )
            part = parts[0].astype(jnp.float32)
            for mask, sent in zip(masks[1:], parts[1:]):
                part = part + swap(sent, mask).astype(jnp.float32)
            sums.append(part.astype(jnp.bfloat16) if k else part)
        total = sums[-1]
        for k, part in zip(TURNS[:-1], sums):
            total = total + swap(part, k * plane).astype(jnp.float32)
        back = swap(dq_t[:, local:].T.astype(jnp.bfloat16), 1)
        own = dq_t[:, :local].T.astype(jnp.bfloat16)
        grad_queries = jnp.concatenate(
            [jnp.where(side == 0, own, back), jnp.where(side == 0, back, own)], axis=1
        )
    else:
        kv = lax.all_gather(kv_local, BOTH, axis=0, tiled=True)
        device = jnp.arange(count, dtype=jnp.int32)
        plan = make_plan(device, mine, span_order, local, span, device)
        dkv, dq_t = attend(plan, kv, local, q_t, d_t, q, do, lse, delta, dq_t, span, 1, jnp.float32)
        total = lax.psum_scatter(dkv, BOTH, scatter_dimension=0, tiled=True)
        grad_queries = lax.all_to_all(dq_t.T.astype(jnp.bfloat16), "uly", split_axis=0, concat_axis=1, tiled=True)
    total = total.astype(jnp.bfloat16)
    return (grad_queries, total[:, :head_dim], total[:, head_dim:])


def solution(mesh):
    return jax.shard_map(
        body,
        mesh=mesh,
        in_specs=(
            P(BOTH, None),
            P(BOTH, None),
            P(BOTH, None),
            P(BOTH, None),
            P(BOTH, None),
            P(None, BOTH),
            P(),
        ),
        out_specs=(P(BOTH, None), P(BOTH, None), P(BOTH, None)),
        check_vma=False,
    )
```
